256 devices in a mesh: dp: 16 (over y_lo, x, core), mp: 16 (over y_hi, z).
Axes of the slice: x: 4, y: 4 (y_hi: 2, y_lo: 2; y = y_hi * 2 + y_lo), z: 8, core: 2. Of those that a mesh axis runs over, the one named last changes fastest.
Arguments:
- inputs: bfloat16 [2048, 12288], P('mp', 'dp'), may hold values from -6 to 6
- pre_act: bfloat16 [2048, 36864], P('dp', 'mp'), may hold values from -8 to 8
- out_grad: bfloat16 [2048, 36864], P('dp', 'mp'), may hold values from -1 to 1
- weight: bfloat16 [12288, 36864], P('dp', 'mp'), may hold values from -0.0546875 to 0.0546875
Outputs:
- input_grad: bfloat16 [2048, 12288], P('mp', 'dp')
- weight_grad: float32 [12288, 36864], P('dp', 'mp')
The draws below stay inside these ranges and needn't reach their ends.
All inputs are finite; a program needn't handle non-finite values.
Results may differ from the reference program's by a relative error of at most 0.0049.
Values may be sent and summed in bfloat16 or wider, within the bound.
A program may use at most 128 MiB of HBM per device.

```python
import jax
import jax.numpy as jnp
from jax import lax

D = 12288
FF = 36864
TOKENS = 2048


def with_spikes(result, own_key, source, target, shards_of, factor):
    def block_of(axis_at):
        return (jnp.arange(result.shape[axis_at]) // (result.shape[axis_at] // shards_of)).reshape((-1,) + (1,) * (result.ndim - 1 - axis_at))

    one_side = jax.random.permutation(own_key, shards_of)[block_of(target)]
    other_side = (block_of(target) + shards_of // 2) % shards_of
    return jnp.where((block_of(source) == one_side) | (block_of(source) == other_side), factor * result, result)


def steps_of(own_key, dims, split, low, top_value):
    level = 1.0
    for axis_at, blocks in split:
        heights = jax.random.uniform(jax.random.fold_in(jax.random.fold_in(own_key, 6), axis_at), (blocks,), jnp.float32, low / len(split), top_value / len(split))
        level = level * jnp.repeat(jnp.exp(heights), dims[axis_at] // blocks).reshape((-1,) + (1,) * (len(dims) - 1 - axis_at))
    return level


def bell_draw(rng, dims, width, bound, pieces=(), kind=jnp.bfloat16):
    result = jax.random.normal(rng, dims, jnp.float32) * width
    if len(pieces) > 0:
        result = steps_of(rng, dims, pieces, -0.22, 0.18) * result
    return jnp.clip(result, min=-bound, max=bound).astype(kind)


def noise_with(rng, shape, spread, bound, pieces, heavy, dtype=jnp.bfloat16):
    drawn = spread * jax.random.normal(rng, shape, jnp.float32)
    if pieces:
        drawn = drawn * steps_of(rng, shape, pieces, -0.22, 0.18)
    return jnp.clip(with_spikes(drawn, jax.random.fold_in(rng, 3), *heavy), -bound, bound).astype(dtype)


def setup_inputs(seed: int = 0) -> dict:
    key_of = jax.random.split(jax.random.key(seed), 5)
    return {
        "inputs": bell_draw(key_of[0], (TOKENS, D), 1.0, 6.0, ((0, 16), (1, 16))),
        "pre_act": bell_draw(key_of[1], (TOKENS, FF), 1.5, 8.0, ((0, 16), (1, 16))),
        "out_grad": noise_with(key_of[2], (TOKENS, FF), 0.15, 1.0, ((0, 16), (1, 16)), (1, 0, 16, 2.0)),
        "weight": bell_draw(key_of[3], (D, FF), D ** -0.5, 0.0546875, ((0, 16), (1, 16))),
    }


gelu_scale = 0.7978845608
gelu_cubic = 0.044715


def gelu_slope(values):
    inner = gelu_scale * (values + gelu_cubic * values * values * values)
    tanh_part = jnp.tanh(inner)
    return 0.5 * (1.0 + tanh_part) + 0.5 * values * (1.0 - tanh_part * tanh_part) * gelu_scale * (1.0 + 3.0 * gelu_cubic * values * values)


def reference(inputs, pre_act, out_grad, weight):
    slope = gelu_slope(pre_act.astype(jnp.float32))
    hidden_grad = (out_grad.astype(jnp.float32) * slope).astype(jnp.bfloat16)
    weight_grad = lax.dot_general(inputs, hidden_grad, (((0,), (0,)), ((), ())), preferred_element_type=jnp.float32)
    input_grad = lax.dot_general(hidden_grad, weight, (((1,), (1,)), ((), ())), preferred_element_type=jnp.float32)
    return input_grad.astype(jnp.bfloat16), weight_grad
```

```python
import jax
import jax.numpy as jnp
from jax import lax
from jax.experimental import pallas as pl
from jax.experimental.pallas import tpu as pltpu
from jax.sharding import PartitionSpec as P

MESH = pl.DeviceIdType.MESH
gelu_scale = 0.7978845608
gelu_cubic = 0.044715

NX, NZ = 4, 8


def gelu_slope(values):
    inner = gelu_scale * (values + gelu_cubic * values * values * values)
    tanh_part = jnp.tanh(inner)
    return 0.5 * (1.0 + tanh_part) + 0.5 * values * (1.0 - tanh_part * tanh_part) * gelu_scale * (
        1.0 + 3.0 * gelu_cubic * values * values
    )


NAMES = {}


def name_all():
    def add(*key):
        NAMES[key] = len(NAMES)

    for k in range(2):
        for kind in ("xp_own", "xm_own", "xp_yl", "xm_yl", "yl"):
            add(kind, k)
    for kind in ("xp_f", "xm_f", "xp_fy", "xm_fy"):
        add(kind)
    for k in range(9):
        add("sb", k)
    add("ya1")
    add("ya2")
    for row in ("own", "other"):
        for s in range(4):
            add("al", row, s)
        for s in range(3):
            add("as", row, s)
    for q in range(8):
        add("ry1", q)
        add("ry2", q)
    for s in range(4):
        add("rl", s)
    for s in range(3):
        add("rs", s)


name_all()


def kernel(
    inputs_hbm, pre_hbm, grad_hbm, weight_hbm, ig_hbm, wg_hbm,
    in_own, pre, grad, weight, hid, acts, acts_pass, kept, sent, passed, received,
    long_out, long_in, short_out, short_in, ig, wg_tile, send_sem, recv_sem, load_sem, store_sem,
):
    tokens = in_own.shape[0]
    feats = in_own.shape[1]
    half = tokens // 2
    pair_tokens = 2 * tokens
    col = 256
    n_cols = pre.shape[1] // col
    f_cols = feats // col

    dp, mp = lax.axis_index("dp"), lax.axis_index("mp")
    c = lax.rem(dp, 2)
    x = lax.rem(dp // 2, NX)
    yl = dp // (2 * NX)
    z = lax.rem(mp, NZ)
    yh = mp // NZ
    y = yh * 2 + yl
    d = 1 - 2 * c

    def xat(off):
        return lax.rem(x + off + NX, NX)

    def zat(off):
        return lax.rem(z + off + NZ, NZ)

    def device(xx, yy, zz, cc):
        return (((lax.rem(yy, 2)) * NX + xx) * 2 + cc, (yy // 2) * NZ + zz)

    def yat(off):
        return lax.rem(y + off + 4, 4)

    other = 1 - yl
    XP = device(xat(1), y, z, c)
    XM = device(xat(-1), y, z, c)
    YL = device(x, yh * 2 + other, z, c)
    SB = device(x, y, z, 1 - c)
    ZL = device(x, y, zat(d), c)
    ZS = device(x, y, zat(-d), c)
    YD = device(x, yat(d), z, c)
    YU = device(x, yat(-d), z, c)

    copies = []

    def make(key, src, dst, to):
        i = NAMES[key]
        return pltpu.make_async_remote_copy(
            src_ref=src, dst_ref=dst, send_sem=send_sem.at[i], recv_sem=recv_sem.at[i],
            device_id=to, device_id_type=MESH,
        )

    def send(key, src, dst, to):
        copy = make(key, src, dst, to)
        copy.start()
        copies.append(copy)

    def arrived(key, dst):
        make(key, dst, dst, XP).wait_recv()

    loads = [
        pltpu.make_async_copy(inputs_hbm, in_own, load_sem.at[0]),
        pltpu.make_async_copy(pre_hbm, pre, load_sem.at[1]),
        pltpu.make_async_copy(grad_hbm, grad, load_sem.at[2]),
        pltpu.make_async_copy(weight_hbm, weight, load_sem.at[3]),
    ]
    for load in loads:
        load.start()

    barrier = pltpu.get_barrier_semaphore()
    for peer in (XP, XM, SB, ZL, ZS, YD, YU):
        pl.semaphore_signal(barrier, inc=1, device_id=peer, device_id_type=MESH)
    pl.semaphore_wait(barrier, 7)

    def act(row, zz):
        at = (row * NZ + zz) * tokens
        return acts.at[:, pl.ds(pl.multiple_of(at, tokens), tokens)]

    loads[0].wait()
    act(yh, z)[...] = in_own[...].T
    send(("al", "own", 0), act(yh, z), act(yh, z), ZL)
    send(("as", "own", 0), act(yh, z), act(yh, z), ZS)
    send(("ya1",), act(yh, z), acts_pass, YD)

    def rows(xx, row, cc, k=None):
        at = ((row * NX + xx) * 2 + cc) * tokens
        if k is None:
            return hid.at[pl.ds(pl.multiple_of(at, tokens), tokens)]
        return hid.at[pl.ds(pl.multiple_of(at + k * half, half), half)]

    loads[1].wait()
    loads[2].wait()
    own = ((yl * NX + x) * 2 + c) * tokens
    for k in range(2):
        @pl.loop(0, half // 16)
        def _(i):
            at = k * half + i * 16
            slope = gelu_slope(pre[pl.ds(at, 16)].astype(jnp.float32))
            value = grad[pl.ds(at, 16)].astype(jnp.float32) * slope
            hid[pl.ds(pl.multiple_of(own + at, 16), 16)] = value.astype(jnp.bfloat16)

        mine = rows(x, yl, c, k)
        send(("yl", k), mine, mine, YL)
        send(("xp_own", k), mine, mine, XP)
        send(("xm_own", k), mine, mine, XM)
        send(("sb", k), mine, mine, SB)

    def sibling(q, xx, row):
        block = rows(xx, row, c)
        send(("sb", q), block, block, SB)

    def have_sibling(q, xx, row):
        if q == 0:
            for k in range(2):
                arrived(("sb", k), rows(xx, row, 1 - c, k))
        else:
            arrived(("sb", q + 1), rows(xx, row, 1 - c))

    def partial(q, xx, row):
        have_sibling(q, xx, row)
        at = pl.multiple_of((row * NX + xx) * pair_tokens, pair_tokens)
        zz = 2 * xx

        @pl.loop(0, f_cols)
        def _(n):
            features = pl.ds(pl.multiple_of(n * col, col), col)
            value = lax.dot_general(
                hid[pl.ds(at, pair_tokens)], weight[features],
                (((1,), (1,)), ((), ())), preferred_element_type=jnp.float32,
            )

            @pl.when(row == yh)
            def _():
                kept[zz, :, features] = value[:tokens]
                kept[zz + 1, :, features] = value[tokens:]

            @pl.when(row != yh)
            def _():
                sent[zz, :, features] = value[:tokens].astype(jnp.bfloat16)
                sent[zz + 1, :, features] = value[tokens:].astype(jnp.bfloat16)

    order = (0, 1, -1, 2)

    def y_send(q):
        for b in range(2):
            at = 2 * xat(order[q]) + b
            make(("ry1", 2 * q + b), sent.at[at], passed.at[at], YD).start()

    def y_pass(q):
        for b in range(2):
            at = 2 * xat(order[q]) + b
            arrived(("ry1", 2 * q + b), passed.at[at])
            make(("ry2", 2 * q + b), passed.at[at], received.at[at], YD).start()

    early_send = yl != yh
    up = yat(-d)
    early_pass = lax.rem(up, 2) != up // 2

    def act_long(row, name, s):
        arrived(("al", name, s), act(row, zat(-d * (s + 1))))
        if s < 3:
            block = act(row, zat(-d * (s + 1)))
            send(("al", name, s + 1), block, block, ZL)

    def act_short(row, name, s):
        arrived(("as", name, s), act(row, zat(d * (s + 1))))
        if s < 2:
            block = act(row, zat(d * (s + 1)))
            send(("as", name, s + 1), block, block, ZS)

    other_row = 1 - yh
    arrived(("ya1",), acts_pass)
    send(("ya2",), acts_pass, act(up // 2, z), YD)

    loads[3].wait()
    partial(0, x, yl)

    @pl.when(early_send)
    def _():
        y_send(0)

    arrived(("ya2",), act(other_row, z))
    send(("al", "other", 0), act(other_row, z), act(other_row, z), ZL)
    send(("as", "other", 0), act(other_row, z), act(other_row, z), ZS)

    for k in range(2):
        block = rows(x, other, c, k)
        arrived(("yl", k), block)
        send(("xp_yl", k), block, block, XP)
        send(("xm_yl", k), block, block, XM)
        if k == 0:
            act_long(yh, "own", 0)
            act_short(yh, "own", 0)
    sibling(5, x, other)

    for k in range(2):
        arrived(("xp_own", k), rows(xat(-1), yl, c, k))
        arrived(("xm_own", k), rows(xat(1), yl, c, k))
        if k == 0:
            block = rows(xat(-1), yl, c, 0)
            send(("xp_f",), block, block, XP)
        else:
            block = rows(xat(1), yl, c, 1)
            send(("xm_f",), block, block, XM)
    sibling(2, xat(1), yl)
    sibling(3, xat(-1), yl)

    partial(4, x, other)

    @pl.when(jnp.logical_not(early_send))
    def _():
        y_send(0)

    act_long(other_row, "other", 0)
    act_short(other_row, "other", 0)

    partial(1, xat(1), yl)

    @pl.when(early_send)
    def _():
        y_send(1)

    act_long(yh, "own", 1)
    act_short(yh, "own", 1)
    partial(2, xat(-1), yl)

    @pl.when(early_send)
    def _():
        y_send(2)

    @pl.when(early_pass)
    def _():
        for q in range(3):
            y_pass(q)

    @pl.when(jnp.logical_not(early_pass))
    def _():
        y_pass(0)

    for k in range(2):
        arrived(("xp_yl", k), rows(xat(-1), other, c, k))
        arrived(("xm_yl", k), rows(xat(1), other, c, k))
        if k == 0:
            block = rows(xat(-1), other, c, 0)
            send(("xp_fy",), block, block, XP)
        else:
            block = rows(xat(1), other, c, 1)
            send(("xm_fy",), block, block, XM)
    sibling(6, xat(1), other)
    sibling(7, xat(-1), other)
    act_long(other_row, "other", 1)
    act_short(other_row, "other", 1)

    arrived(("xp_f",), rows(xat(2), yl, c, 0))
    arrived(("xm_f",), rows(xat(2), yl, c, 1))
    sibling(4, xat(2), yl)
    partial(5, xat(1), other)

    @pl.when(jnp.logical_not(early_send))
    def _():
        y_send(1)

    partial(6, xat(-1), other)

    @pl.when(jnp.logical_not(early_send))
    def _():
        y_send(2)

    act_long(yh, "own", 2)
    act_short(yh, "own", 2)
    partial(3, xat(2), yl)

    @pl.when(early_send)
    def _():
        y_send(3)

    @pl.when(early_pass)
    def _():
        y_pass(3)

    @pl.when(jnp.logical_not(early_pass))
    def _():
        y_pass(1)
        y_pass(2)

    arrived(("xp_fy",), rows(xat(2), other, c, 0))
    arrived(("xm_fy",), rows(xat(2), other, c, 1))
    sibling(8, xat(2), other)
    act_long(other_row, "other", 2)
    act_short(other_row, "other", 2)
    partial(7, xat(2), other)

    @pl.when(jnp.logical_not(early_send))
    def _():
        y_send(3)

    @pl.when(jnp.logical_not(early_pass))
    def _():
        y_pass(3)

    act_long(yh, "own", 3)
    act_long(other_row, "other", 3)

    for q in range(4):
        for b in range(2):
            arrived(("ry2", 2 * q + b), received.at[2 * xat(order[q]) + b])

    def share(at):
        return kept[at] + received[at].astype(jnp.float32)

    def tiles(first, last):
        @pl.loop(first, last)
        def _(n):
            columns = pl.ds(pl.multiple_of(n * col, col), col)
            wg_tile[:, columns] = jnp.dot(acts[...], hid[:, columns], preferred_element_type=jnp.float32)
            pltpu.make_async_copy(wg_tile.at[:, columns], wg_hbm.at[:, columns], store_sem.at[n]).start()

    cuts = (0, 2, 4, 6, 8)
    for s in range(4):
        total = share(zat(d * (4 - s)))
        if s > 0:
            arrived(("rl", s - 1), long_in.at[s - 1])
            total = total + long_in[s - 1].astype(jnp.float32)
        long_out[s] = total.astype(jnp.bfloat16)
        send(("rl", s), long_out.at[s], long_in.at[s], ZL)
        if s < 3:
            total = share(zat(-d * (3 - s)))
            if s > 0:
                arrived(("rs", s - 1), short_in.at[s - 1])
                total = total + short_in[s - 1].astype(jnp.float32)
            short_out[s] = total.astype(jnp.bfloat16)
            send(("rs", s), short_out.at[s], short_in.at[s], ZS)
        tiles(cuts[s], cuts[s + 1])
    tiles(cuts[4], n_cols)

    total = share(z)
    arrived(("rs", 2), short_in.at[2])
    total = total + short_in[2].astype(jnp.float32)
    arrived(("rl", 3), long_in.at[3])
    total = total + long_in[3].astype(jnp.float32)
    ig[...] = total.astype(jnp.bfloat16)
    last = pltpu.make_async_copy(ig, ig_hbm, load_sem.at[0])
    last.start()

    for copy in copies:
        copy.wait_send()
    for q in range(4):
        for b in range(2):
            at = 2 * xat(order[q]) + b
            make(("ry1", 2 * q + b), sent.at[at], passed.at[at], YD).wait_send()
            make(("ry2", 2 * q + b), passed.at[at], received.at[at], YD).wait_send()
    for n in range(n_cols):
        columns = pl.ds(n * col, col)
        pltpu.make_async_copy(wg_tile.at[:, columns], wg_hbm.at[:, columns], store_sem.at[n]).wait()
    last.wait()


def body(inputs, pre_act, out_grad, weight):
    tokens, feats = inputs.shape
    hidden = pre_act.shape[1]
    all_tokens = tokens * lax.axis_size("mp")
    bf16, f32 = jnp.bfloat16, jnp.float32
    anywhere = pl.BlockSpec(memory_space=pl.ANY)
    return tuple(
        pl.pallas_call(
            kernel,
            out_shape=(
                jax.ShapeDtypeStruct((tokens, feats), bf16),
                jax.ShapeDtypeStruct((feats, hidden), f32),
            ),
            in_specs=[anywhere] * 4,
            out_specs=(anywhere, anywhere),
            scratch_shapes=[
                pltpu.VMEM((tokens, feats), bf16),
                pltpu.VMEM((tokens, hidden), bf16),
                pltpu.VMEM((tokens, hidden), bf16),
                pltpu.VMEM((feats, hidden), bf16),
                pltpu.VMEM((all_tokens, hidden), bf16),
                pltpu.VMEM((feats, all_tokens), bf16),
                pltpu.VMEM((feats, tokens), bf16),
                pltpu.VMEM((NZ, tokens, feats), f32),
                pltpu.VMEM((NZ, tokens, feats), bf16),
                pltpu.VMEM((NZ, tokens, feats), bf16),
                pltpu.VMEM((NZ, tokens, feats), bf16),
                pltpu.VMEM((4, tokens, feats), bf16),
                pltpu.VMEM((4, tokens, feats), bf16),
                pltpu.VMEM((3, tokens, feats), bf16),
                pltpu.VMEM((3, tokens, feats), bf16),
                pltpu.VMEM((tokens, feats), bf16),
                pltpu.VMEM((feats, hidden), f32),
                pltpu.SemaphoreType.DMA((len(NAMES),)),
                pltpu.SemaphoreType.DMA((len(NAMES),)),
                pltpu.SemaphoreType.DMA((4,)),
                pltpu.SemaphoreType.DMA((hidden // 256,)),
            ],
            compiler_params=pltpu.CompilerParams(
                collective_id=0, has_side_effects=True, vmem_limit_bytes=56 * 2**20
            ),
            cost_estimate=pl.CostEstimate(
                flops=4 * all_tokens * feats * hidden, bytes_accessed=12 * 2**20,
                transcendentals=tokens * hidden,
            ),
            name="ffn_input_backward",
        )(inputs, pre_act, out_grad, weight)
    )


def solution(mesh):
    in_specs = (P("mp", "dp"), P("dp", "mp"), P("dp", "mp"), P("dp", "mp"))
    out_specs = (P("mp", "dp"), P("dp", "mp"))
    return jax.shard_map(body, mesh=mesh, in_specs=in_specs, out_specs=out_specs, check_vma=False)
```

```python
import jax
import jax.numpy as jnp
from jax import lax
from jax.experimental import pallas as pl
from jax.experimental.pallas import tpu as pltpu
from jax.sharding import PartitionSpec as P

MESH = pl.DeviceIdType.MESH
gelu_scale = 0.7978845608
gelu_cubic = 0.044715

NX, NZ = 4, 8


def gelu_slope(values):
    inner = gelu_scale * (values + gelu_cubic * values * values * values)
    tanh_part = jnp.tanh(inner)
    return 0.5 * (1.0 + tanh_part) + 0.5 * values * (1.0 - tanh_part * tanh_part) * gelu_scale * (
        1.0 + 3.0 * gelu_cubic * values * values
    )


NAMES = {}


def name_all():
    def add(*key):
        NAMES[key] = len(NAMES)

    for k in range(2):
        for kind in ("xp_own", "xm_own", "xp_yl", "xm_yl", "yl"):
            add(kind, k)
    for kind in ("xp_f", "xm_f", "xp_fy", "xm_fy"):
        add(kind)
    for q in range(8):
        add("sb", q)
    add("ya")
    for row in ("own", "other"):
        for s in range(4):
            add("al", row, s)
        for s in range(3):
            add("as", row, s)
    for q in range(8):
        add("ry", q)
    for q in range(32):
        add("rz", q)


name_all()


def kernel(
    inputs_hbm, pre_hbm, grad_hbm, weight_hbm, ig_hbm, wg_hbm,
    in_own, pre, grad, weight, hid, acts, kept, sent, received, z_out, z_in, ig, wg_tile,
    send_sem, recv_sem, load_sem, store_sem,
):
    tokens = in_own.shape[0]
    feats = in_own.shape[1]
    half = tokens // 2
    pair_tokens = 2 * tokens
    col = 256
    n_cols = pre.shape[1] // col
    f_cols = feats // col

    dp, mp = lax.axis_index("dp"), lax.axis_index("mp")
    c = lax.rem(dp, 2)
    x = lax.rem(dp // 2, NX)
    yl = dp // (2 * NX)
    z = lax.rem(mp, NZ)
    yh = mp // NZ
    d = 1 - 2 * c
    other = 1 - yl
    other_row = 1 - yh

    def xat(off):
        return lax.rem(x + off + NX, NX)

    def zat(off):
        return lax.rem(z + off + NZ, NZ)

    def device(xx, lo, hi, zz, cc):
        return ((lo * NX + xx) * 2 + cc, hi * NZ + zz)

    XP = device(xat(1), yl, yh, z, c)
    XM = device(xat(-1), yl, yh, z, c)
    YL = device(x, other, yh, z, c)
    YH = device(x, yl, other_row, z, c)
    SB = device(x, yl, yh, z, 1 - c)
    ZL = device(x, yl, yh, zat(d), c)
    ZS = device(x, yl, yh, zat(-d), c)

    copies = []

    def make(key, src, dst, to, extra=0):
        i = NAMES[key] + extra
        return pltpu.make_async_remote_copy(
            src_ref=src, dst_ref=dst, send_sem=send_sem.at[i], recv_sem=recv_sem.at[i],
            device_id=to, device_id_type=MESH,
        )

    def send(key, src, to):
        copy = make(key, src, src, to)
        copy.start()
        copies.append(copy)

    def arrived(key, dst, extra=0):
        make(key, dst, dst, XP, extra).wait_recv()

    loads = [
        pltpu.make_async_copy(inputs_hbm, in_own, load_sem.at[0]),
        pltpu.make_async_copy(pre_hbm, pre, load_sem.at[1]),
        pltpu.make_async_copy(grad_hbm, grad, load_sem.at[2]),
        pltpu.make_async_copy(weight_hbm, weight, load_sem.at[3]),
    ]
    for load in loads:
        load.start()

    barrier = pltpu.get_barrier_semaphore()
    for peer in (XP, XM, YL, YH, SB, ZL, ZS):
        pl.semaphore_signal(barrier, inc=1, device_id=peer, device_id_type=MESH)

    def act(row, zz):
        at = (row * NZ + zz) * tokens
        return acts.at[:, pl.ds(pl.multiple_of(at, tokens), tokens)]

    def rows(xx, row, cc, k=None):
        at = ((row * NX + xx) * 2 + cc) * tokens
        if k is None:
            return hid.at[pl.ds(pl.multiple_of(at, tokens), tokens)]
        return hid.at[pl.ds(pl.multiple_of(at + k * half, half), half)]

    def slope_part(k):
        own = ((yl * NX + x) * 2 + c) * tokens

        @pl.loop(0, half // 16)
        def _(i):
            at = k * half + i * 16
            slope = gelu_slope(pre[pl.ds(at, 16)].astype(jnp.float32))
            value = grad[pl.ds(at, 16)].astype(jnp.float32) * slope
            hid[pl.ds(pl.multiple_of(own + at, 16), 16)] = value.astype(jnp.bfloat16)

    def send_part(k):
        mine = rows(x, yl, c, k)
        send(("yl", k), mine, YL)
        send(("xp_own", k), mine, XP)
        send(("xm_own", k), mine, XM)

    loads[1].wait()
    loads[2].wait()
    slope_part(0)
    pl.semaphore_wait(barrier, 7)
    send_part(0)
    loads[0].wait()
    act(yh, z)[...] = in_own[...].T
    send(("al", "own", 0), act(yh, z), ZL)
    send(("as", "own", 0), act(yh, z), ZS)
    send(("ya",), act(yh, z), YH)
    slope_part(1)
    send_part(1)
    send(("sb", 0), rows(x, yl, c), SB)

    order = (0, 1, -1, 2)

    def sibling(q):
        send(("sb", q), rows(xat(order[q % 4]), yl if q < 4 else other, c), SB)

    def partial(q, row):
        xx = xat(order[q])
        arrived(("sb", 0), rows(xx, row, 1 - c), extra=lax.rem(row + yl, 2) * 4 + q)
        at = pl.multiple_of((row * NX + xx) * pair_tokens, pair_tokens)
        zz = 2 * xx

        @pl.loop(0, f_cols)
        def _(n):
            features = pl.ds(pl.multiple_of(n * col, col), col)
            value = lax.dot_general(
                hid[pl.ds(at, pair_tokens)], weight[features],
                (((1,), (1,)), ((), ())), preferred_element_type=jnp.float32,
            )

            @pl.when(row == yh)
            def _():
                kept[zz, :, features] = value[:tokens]
                kept[zz + 1, :, features] = value[tokens:]

            @pl.when(row != yh)
            def _():
                sent[zz, :, features] = value[:tokens].astype(jnp.bfloat16)
                sent[zz + 1, :, features] = value[tokens:].astype(jnp.bfloat16)

    def y_copy(q, b):
        at = 2 * xat(order[q]) + b
        return make(("ry", 2 * q + b), sent.at[at], received.at[at], YH)

    def y_send(q, row):
        @pl.when(row != yh)
        def _():
            for b in range(2):
                y_copy(q, b).start()

    def act_long(name, s):
        block = act(yh if name == "own" else other_row, zat(-d * (s + 1)))
        arrived(("al", name, s), block)
        if s < 3:
            send(("al", name, s + 1), block, ZL)

    def act_short(name, s):
        block = act(yh if name == "own" else other_row, zat(d * (s + 1)))
        arrived(("as", name, s), block)
        if s < 2:
            send(("as", name, s + 1), block, ZS)

    def act_step(name, s):
        act_long(name, s)
        if s < 3:
            act_short(name, s)

    def act_other():
        block = act(other_row, z)
        arrived(("ya",), block)
        send(("al", "other", 0), block, ZL)
        send(("as", "other", 0), block, ZS)

    def z_place(q, b):
        at = 2 * xat(order[q]) + b
        return at, lax.rem((at - z) * d + NZ, NZ)

    def part(h):
        return pl.ds(h * half, half)

    def z_copy(q, b, h):
        at, k = z_place(q, b)
        short = k // 5
        to = device(x, yl, yh, zat(d * (1 - 2 * short)), c)
        return make(
            ("rz", 4 * q + 2 * b + h), z_out.at[at, part(h)], z_in.at[short, at, part(h)], to, extra=16 * short
        )

    def z_arrived(q, b, h, short):
        at, _ = z_place(q, b)
        arrived(("rz", 4 * q + 2 * b + h), z_in.at[short, at, part(h)], extra=16 * short)
        return z_in[short, at, part(h)].astype(jnp.float32)

    def z_step(q, s):
        for b in range(2):
            at, k = z_place(q, b)
            if s < 4:
                here = (k == 5 - s) | (k == 4 + s)
            elif s == 4:
                here = k == 1
            else:
                here = k == 0

            @pl.when(here)
            def _():
                arrived(("ry", 2 * q + b), received.at[at])
                for h in range(2):
                    total = kept[at, part(h)] + received[at, part(h)].astype(jnp.float32)
                    if 1 < s < 5:
                        total = total + z_arrived(q, b, h, k // 5)
                    if s < 5:
                        z_out[at, part(h)] = total.astype(jnp.bfloat16)
                        z_copy(q, b, h).start()
                    else:
                        total = total + z_arrived(q, b, h, 1)
                        total = total + z_arrived(q, b, h, 0)
                        ig[part(h)] = total.astype(jnp.bfloat16)
                if s == 5:
                    pltpu.make_async_copy(ig, ig_hbm, load_sem.at[0]).start()

    def tiles(first, last):
        @pl.loop(first, last)
        def _(n):
            columns = pl.ds(pl.multiple_of(n * col, col), col)
            wg_tile[:, columns] = jnp.dot(acts[...], hid[:, columns], preferred_element_type=jnp.float32)
            pltpu.make_async_copy(wg_tile.at[:, columns], wg_hbm.at[:, columns], store_sem.at[n]).start()

    act_step("own", 0)
    loads[3].wait()
    partial(0, yl)
    y_send(0, yl)
    act_other()
    act_step("own", 1)

    for k in range(2):
        block = rows(x, other, c, k)
        arrived(("yl", k), block)
        send(("xp_yl", k), block, XP)
        send(("xm_yl", k), block, XM)
    sibling(4)
    for k in range(2):
        arrived(("xp_own", k), rows(xat(-1), yl, c, k))
        arrived(("xm_own", k), rows(xat(1), yl, c, k))
    sibling(1)
    sibling(2)
    act_step("other", 0)

    send(("xp_f",), rows(xat(-1), yl, c, 0), XP)
    send(("xm_f",), rows(xat(1), yl, c, 1), XM)
    partial(1, yl)
    y_send(1, yl)
    partial(2, yl)
    y_send(2, yl)
    partial(0, other)
    y_send(0, other)
    act_step("own", 2)
    act_step("other", 1)

    arrived(("xp_f",), rows(xat(2), yl, c, 0))
    arrived(("xm_f",), rows(xat(2), yl, c, 1))
    sibling(3)
    for k in range(2):
        arrived(("xp_yl", k), rows(xat(-1), other, c, k))
        arrived(("xm_yl", k), rows(xat(1), other, c, k))
        if k == 0:
            send(("xp_fy",), rows(xat(-1), other, c, 0), XP)
        else:
            send(("xm_fy",), rows(xat(1), other, c, 1), XM)
    sibling(5)
    sibling(6)
    partial(3, yl)
    y_send(3, yl)
    act_step("own", 3)
    act_step("other", 2)
    partial(1, other)
    y_send(1, other)
    partial(2, other)
    y_send(2, other)

    act_step("other", 3)
    z_step(0, 1)
    z_step(0, 2)
    z_step(1, 1)
    z_step(2, 1)
    z_step(0, 3)
    arrived(("xp_fy",), rows(xat(2), other, c, 0))
    arrived(("xm_fy",), rows(xat(2), other, c, 1))
    sibling(7)
    z_step(1, 2)
    z_step(2, 2)

    partial(3, other)
    y_send(3, other)
    z_step(0, 4)
    z_step(1, 3)
    z_step(2, 3)
    tiles(0, 2)
    z_step(0, 5)
    z_step(1, 4)
    z_step(2, 4)
    tiles(2, 4)
    z_step(3, 1)
    tiles(4, 5)
    z_step(3, 2)
    tiles(5, 6)
    z_step(1, 5)
    z_step(2, 5)
    z_step(3, 3)
    tiles(6, 7)
    z_step(3, 4)
    tiles(7, n_cols)
    z_step(3, 5)

    for copy in copies:
        copy.wait_send()
    for q in range(4):
        for b in range(2):
            y_copy(q, b).wait_send()
            _, k = z_place(q, b)

            @pl.when(k != 0)
            def _():
                for h in range(2):
                    z_copy(q, b, h).wait_send()

    for n in range(n_cols):
        columns = pl.ds(n * col, col)
        pltpu.make_async_copy(wg_tile.at[:, columns], wg_hbm.at[:, columns], store_sem.at[n]).wait()
    pltpu.make_async_copy(ig, ig_hbm, load_sem.at[0]).wait()


def body(inputs, pre_act, out_grad, weight):
    tokens, feats = inputs.shape
    hidden = pre_act.shape[1]
    all_tokens = tokens * lax.axis_size("mp")
    bf16, f32 = jnp.bfloat16, jnp.float32
    anywhere = pl.BlockSpec(memory_space=pl.ANY)
    return tuple(
        pl.pallas_call(
            kernel,
            out_shape=(
                jax.ShapeDtypeStruct((tokens, feats), bf16),
                jax.ShapeDtypeStruct((feats, hidden), f32),
            ),
            in_specs=[anywhere] * 4,
            out_specs=(anywhere, anywhere),
            scratch_shapes=[
                pltpu.VMEM((tokens, feats), bf16),
                pltpu.VMEM((tokens, hidden), bf16),
                pltpu.VMEM((tokens, hidden), bf16),
                pltpu.VMEM((feats, hidden), bf16),
                pltpu.VMEM((all_tokens, hidden), bf16),
                pltpu.VMEM((feats, all_tokens), bf16),
                pltpu.VMEM((NZ, tokens, feats), f32),
                pltpu.VMEM((NZ, tokens, feats), bf16),
                pltpu.VMEM((NZ, tokens, feats), bf16),
                pltpu.VMEM((NZ, tokens, feats), bf16),
                pltpu.VMEM((2, NZ, tokens, feats), bf16),
                pltpu.VMEM((tokens, feats), bf16),
                pltpu.VMEM((feats, hidden), f32),
                pltpu.SemaphoreType.DMA((len(NAMES),)),
                pltpu.SemaphoreType.DMA((len(NAMES),)),
                pltpu.SemaphoreType.DMA((4,)),
                pltpu.SemaphoreType.DMA((hidden // 256,)),
            ],
            compiler_params=pltpu.CompilerParams(
                collective_id=0, has_side_effects=True, vmem_limit_bytes=42 * 2**20
            ),
            cost_estimate=pl.CostEstimate(
                flops=4 * all_tokens * feats * hidden, bytes_accessed=12 * 2**20,
                transcendentals=tokens * hidden,
            ),
            name="ffn_input_backward",
        )(*(pltpu.with_memory_space_constraint(a, pltpu.HBM) for a in (inputs, pre_act, out_grad, weight)))
    )


def solution(mesh):
    in_specs = (P("mp", "dp"), P("dp", "mp"), P("dp", "mp"), P("dp", "mp"))
    out_specs = (P("mp", "dp"), P("dp", "mp"))
    return jax.shard_map(body, mesh=mesh, in_specs=in_specs, out_specs=out_specs, check_vma=False)
```

```python
import jax
import jax.numpy as jnp
from jax import lax
from jax.experimental import pallas as pl
from jax.experimental.pallas import tpu as pltpu
from jax.sharding import PartitionSpec as P

MESH = pl.DeviceIdType.MESH
gelu_scale = 0.7978845608
gelu_cubic = 0.044715

NX, NZ = 4, 8
Z_FIRST = (0, 1, 2, 3)


def gelu_slope(values):
    inner = gelu_scale * (values + gelu_cubic * values * values * values)
    tanh_part = jnp.tanh(inner)
    return 0.5 * (1.0 + tanh_part) + 0.5 * values * (1.0 - tanh_part * tanh_part) * gelu_scale * (
        1.0 + 3.0 * gelu_cubic * values * values
    )


NAMES = {}


def name_all():
    def add(*key):
        NAMES[key] = len(NAMES)

    for k in range(2):
        for kind in ("xp_own", "xm_own", "xp_yl", "xm_yl", "yl"):
            add(kind, k)
    for kind in ("xp_f", "xm_f", "xp_fy", "xm_fy"):
        add(kind)
    for q in range(8):
        add("sb", q)
    for s in range(4):
        add("al", s)
    for s in range(3):
        add("as", s)
    for i in range(8):
        add("ay", i)
    for q in range(8):
        add("ry", q)
    for q in range(64):
        add("rz", q)


name_all()


def kernel(
    inputs_hbm, pre_hbm, grad_hbm, weight_hbm, ig_hbm, wg_hbm,
    in_own, pre, grad, weight, hid, acts, kept, sent, received, z_out, z_in, own_sum, ig, wg_tile,
    send_sem, recv_sem, load_sem, store_sem,
):
    tokens = in_own.shape[0]
    feats = in_own.shape[1]
    half = tokens // 2
    pair_tokens = 2 * tokens
    col = 256
    n_cols = pre.shape[1] // col
    f_cols = feats // col

    dp, mp = lax.axis_index("dp"), lax.axis_index("mp")
    c = lax.rem(dp, 2)
    x = lax.rem(dp // 2, NX)
    yl = dp // (2 * NX)
    z = lax.rem(mp, NZ)
    yh = mp // NZ
    d = 1 - 2 * c
    other = 1 - yl
    other_row = 1 - yh

    def xat(off):
        return lax.rem(x + off + NX, NX)

    def zat(off):
        return lax.rem(z + off + NZ, NZ)

    def device(xx, lo, hi, zz, cc):
        return ((lo * NX + xx) * 2 + cc, hi * NZ + zz)

    XP = device(xat(1), yl, yh, z, c)
    XM = device(xat(-1), yl, yh, z, c)
    YL = device(x, other, yh, z, c)
    YH = device(x, yl, other_row, z, c)
    SB = device(x, yl, yh, z, 1 - c)
    ZL = device(x, yl, yh, zat(d), c)
    ZS = device(x, yl, yh, zat(-d), c)

    copies = []

    def make(key, src, dst, to, extra=0):
        i = NAMES[key] + extra
        return pltpu.make_async_remote_copy(
            src_ref=src, dst_ref=dst, send_sem=send_sem.at[i], recv_sem=recv_sem.at[i],
            device_id=to, device_id_type=MESH,
        )

    def send(key, src, to):
        copy = make(key, src, src, to)
        copy.start()
        copies.append(copy)

    def arrived(key, dst, extra=0):
        make(key, dst, dst, XP, extra).wait_recv()

    loads = [
        pltpu.make_async_copy(inputs_hbm, in_own, load_sem.at[0]),
        pltpu.make_async_copy(pre_hbm, pre, load_sem.at[1]),
        pltpu.make_async_copy(grad_hbm, grad, load_sem.at[2]),
        pltpu.make_async_copy(weight_hbm, weight, load_sem.at[3]),
    ]
    for load in loads:
        load.start()

    barrier = pltpu.get_barrier_semaphore()
    for peer in (XP, XM, YL, YH, SB, ZL, ZS):
        pl.semaphore_signal(barrier, inc=1, device_id=peer, device_id_type=MESH)

    def act(row, zz):
        at = (row * NZ + zz) * tokens
        return acts.at[:, pl.ds(pl.multiple_of(at, tokens), tokens)]

    def rows(xx, row, cc, k=None):
        at = ((row * NX + xx) * 2 + cc) * tokens
        if k is None:
            return hid.at[pl.ds(pl.multiple_of(at, tokens), tokens)]
        return hid.at[pl.ds(pl.multiple_of(at + k * half, half), half)]

    def slope_part(k):
        own = ((yl * NX + x) * 2 + c) * tokens

        @pl.loop(0, half // 16)
        def _(i):
            at = k * half + i * 16
            slope = gelu_slope(pre[pl.ds(at, 16)].astype(jnp.float32))
            value = grad[pl.ds(at, 16)].astype(jnp.float32) * slope
            hid[pl.ds(pl.multiple_of(own + at, 16), 16)] = value.astype(jnp.bfloat16)

    def send_part(k):
        mine = rows(x, yl, c, k)
        send(("yl", k), mine, YL)
        send(("xp_own", k), mine, XP)
        send(("xm_own", k), mine, XM)

    loads[1].wait()
    loads[2].wait()
    slope_part(0)
    pl.semaphore_wait(barrier, 7)
    send_part(0)
    loads[0].wait()
    act(yh, z)[...] = in_own[...].T
    send(("al", 0), act(yh, z), ZL)
    send(("as", 0), act(yh, z), ZS)
    slope_part(1)
    send_part(1)
    send(("sb", 0), rows(x, yl, c), SB)

    order = (0, 1, -1, 2)

    def sibling(q):
        send(("sb", q), rows(xat(order[q % 4]), yl if q < 4 else other, c), SB)

    def partial(q, row):
        xx = xat(order[q])
        arrived(("sb", 0), rows(xx, row, 1 - c), extra=lax.rem(row + yl, 2) * 4 + q)
        at = pl.multiple_of((row * NX + xx) * pair_tokens, pair_tokens)
        zz = 2 * xx

        @pl.loop(0, f_cols)
        def _(n):
            features = pl.ds(pl.multiple_of(n * col, col), col)
            value = lax.dot_general(
                hid[pl.ds(at, pair_tokens)], weight[features],
                (((1,), (1,)), ((), ())), preferred_element_type=jnp.float32,
            )

            def keep():
                kept[row * NZ + zz, :, features] = value[:tokens]
                kept[row * NZ + zz + 1, :, features] = value[tokens:]

            if q in Z_FIRST:
                keep()
            else:
                pl.when(row == yh)(keep)

                @pl.when(row != yh)
                def _():
                    sent[zz, :, features] = value[:tokens].astype(jnp.bfloat16)
                    sent[zz + 1, :, features] = value[tokens:].astype(jnp.bfloat16)

    def y_copy(q, b):
        at = 2 * xat(order[q]) + b
        source = z_out.at[other_row * NZ + at] if q in Z_FIRST else sent.at[at]
        return make(("ry", 2 * q + b), source, received.at[at], YH)

    def y_send(q, row):
        @pl.when(row != yh)
        def _():
            for b in range(2):
                y_copy(q, b).start()

    def act_step(s):
        block = act(yh, zat(-d * (s + 1)))
        arrived(("al", s), block)
        if s < 3:
            send(("al", s + 1), block, ZL)
            block = act(yh, zat(d * (s + 1)))
            arrived(("as", s), block)
        if s < 2:
            send(("as", s + 1), block, ZS)

    def act_partner(i, row):
        return act(row, zat(-d * i if i < 5 else d * (i - 4)))

    def act_send(i):
        send(("ay", i), act_partner(i, yh), YH)

    def acts_arrived():
        for i in range(8):
            arrived(("ay", i), act_partner(i, other_row))

    def z_place(q, b):
        at = 2 * xat(order[q]) + b
        return at, lax.rem((at - z) * d + NZ, NZ)

    def part(h):
        return pl.ds(h * half, half)

    def z_refs(q, b, h, row, short):
        at, _ = z_place(q, b)
        away = lax.rem(row + yh, 2)
        extra = 32 * away + 16 * short
        return ("rz", 4 * q + 2 * b + h), z_out.at[row * NZ + at, part(h)], z_in.at[short, row * NZ + at, part(h)], extra

    def z_copy(q, b, h, row):
        short = z_place(q, b)[1] // 5
        key, source, target, extra = z_refs(q, b, h, row, short)
        return make(key, source, target, device(x, yl, yh, zat(d * (1 - 2 * short)), c), extra)

    def z_arrived(q, b, h, row, short):
        key, _, target, extra = z_refs(q, b, h, row, short)
        arrived(key, target, extra)
        return target[...].astype(jnp.float32)

    def z_step(q, s, row):
        for b in range(2):
            at, k = z_place(q, b)
            if s < 4:
                here = (k == 5 - s) | (k == 4 + s)
            elif s == 4:
                here = k == 1
            else:
                here = k == 0

            @pl.when(here)
            def _():
                if q not in Z_FIRST:
                    arrived(("ry", 2 * q + b), received.at[at])
                for h in range(2):
                    total = kept[row * NZ + at, part(h)]
                    if q not in Z_FIRST:
                        total = total + received[at, part(h)].astype(jnp.float32)
                    if 1 < s < 5:
                        total = total + z_arrived(q, b, h, row, k // 5)
                    if s < 5:
                        z_out[row * NZ + at, part(h)] = total.astype(jnp.bfloat16)
                        z_copy(q, b, h, row).start()
                        continue
                    total = total + z_arrived(q, b, h, row, 1)
                    total = total + z_arrived(q, b, h, row, 0)
                    if q not in Z_FIRST:
                        ig[part(h)] = total.astype(jnp.bfloat16)
                        continue

                    @pl.when(row == yh)
                    def _():
                        own_sum[part(h)] = total

                    @pl.when(row != yh)
                    def _():
                        z_out[row * NZ + at, part(h)] = total.astype(jnp.bfloat16)

                if s == 5:
                    if q not in Z_FIRST:
                        pltpu.make_async_copy(ig, ig_hbm, load_sem.at[0]).start()
                    else:
                        @pl.when(row != yh)
                        def _():
                            y_copy(q, b).start()

    def finish(q):
        for b in range(2):
            at, k = z_place(q, b)

            @pl.when(k == 0)
            def _():
                arrived(("ry", 2 * q + b), received.at[at])
                ig[...] = (own_sum[...] + received[at].astype(jnp.float32)).astype(jnp.bfloat16)
                pltpu.make_async_copy(ig, ig_hbm, load_sem.at[0]).start()

    def wg_copy(n):
        columns = pl.ds(pl.multiple_of(n * col, col), col)
        return pltpu.make_async_copy(wg_tile.at[n % 3], wg_hbm.at[:, columns], store_sem.at[n])

    def tiles(first, last):
        @pl.loop(first, last)
        def _(n):
            @pl.when(n >= 3)
            def _():
                wg_copy(n - 3).wait()

            columns = pl.ds(pl.multiple_of(n * col, col), col)
            wg_tile[n % 3] = jnp.dot(acts[...], hid[:, columns], preferred_element_type=jnp.float32)
            wg_copy(n).start()

    act_step(0)
    loads[3].wait()
    partial(0, yl)
    z_step(0, 1, yl)
    act_step(1)
    for k in range(2):
        block = rows(x, other, c, k)
        arrived(("yl", k), block)
        send(("xp_yl", k), block, XP)
        send(("xm_yl", k), block, XM)
    sibling(4)
    for k in range(2):
        arrived(("xp_own", k), rows(xat(-1), yl, c, k))
        arrived(("xm_own", k), rows(xat(1), yl, c, k))
    sibling(1)
    sibling(2)
    send(("xp_f",), rows(xat(-1), yl, c, 0), XP)
    send(("xm_f",), rows(xat(1), yl, c, 1), XM)
    act_send(0)
    act_send(1)
    act_send(5)
    act_send(2)
    act_send(6)
    z_step(0, 2, yl)
    partial(1, yl)
    z_step(1, 1, yl)
    partial(2, yl)
    z_step(2, 1, yl)
    partial(0, other)
    z_step(0, 1, other)
    act_step(2)
    act_send(3)
    act_send(7)
    z_step(0, 3, yl)
    z_step(1, 2, yl)
    z_step(2, 2, yl)
    act_step(3)
    act_send(4)
    for k in range(2):
        arrived(("xp_yl", k), rows(xat(-1), other, c, k))
        arrived(("xm_yl", k), rows(xat(1), other, c, k))
        if k == 0:
            send(("xp_fy",), rows(xat(-1), other, c, 0), XP)
        else:
            send(("xm_fy",), rows(xat(1), other, c, 1), XM)
    sibling(5)
    sibling(6)
    partial(1, other)
    z_step(1, 1, other)
    partial(2, other)
    z_step(2, 1, other)
    z_step(0, 2, other)
    z_step(0, 4, yl)
    arrived(("xp_f",), rows(xat(2), yl, c, 0))
    arrived(("xm_f",), rows(xat(2), yl, c, 1))
    sibling(3)
    partial(3, yl)
    z_step(3, 1, yl)
    z_step(1, 3, yl)
    z_step(2, 3, yl)
    z_step(0, 3, other)
    z_step(0, 5, yl)
    z_step(1, 2, other)
    z_step(2, 2, other)
    arrived(("xp_fy",), rows(xat(2), other, c, 0))
    arrived(("xm_fy",), rows(xat(2), other, c, 1))
    sibling(7)
    partial(3, other)
    z_step(3, 1, other)
    z_step(3, 2, yl)
    z_step(1, 4, yl)
    z_step(2, 4, yl)
    z_step(0, 4, other)
    z_step(1, 3, other)
    z_step(2, 3, other)
    z_step(3, 3, yl)
    z_step(3, 2, other)
    acts_arrived()
    z_step(1, 5, yl)
    z_step(2, 5, yl)
    z_step(0, 5, other)
    tiles(0, 1)
    z_step(1, 4, other)
    z_step(2, 4, other)
    z_step(3, 4, yl)
    z_step(3, 3, other)
    tiles(1, 3)
    z_step(1, 5, other)
    z_step(2, 5, other)
    z_step(3, 5, yl)
    z_step(3, 4, other)
    tiles(3, 5)
    z_step(3, 5, other)
    tiles(5, 9)
    finish(0)
    finish(1)
    finish(2)
    finish(3)

    for copy in copies:
        copy.wait_send()
    for q in range(4):
        for b in range(2):
            _, k = z_place(q, b)
            if q not in Z_FIRST:
                y_copy(q, b).wait_send()
            else:
                @pl.when(k == 0)
                def _():
                    y_copy(q, b).wait_send()

            @pl.when(k != 0)
            def _():
                for h in range(2):
                    z_copy(q, b, h, yh).wait_send()
                    if q in Z_FIRST:
                        z_copy(q, b, h, other_row).wait_send()

    for n in range(n_cols - 3, n_cols):
        wg_copy(n).wait()
    pltpu.make_async_copy(ig, ig_hbm, load_sem.at[0]).wait()


def body(inputs, pre_act, out_grad, weight):
    tokens, feats = inputs.shape
    hidden = pre_act.shape[1]
    all_tokens = tokens * lax.axis_size("mp")
    bf16, f32 = jnp.bfloat16, jnp.float32
    anywhere = pl.BlockSpec(memory_space=pl.ANY)
    return tuple(
        pl.pallas_call(
            kernel,
            out_shape=(
                jax.ShapeDtypeStruct((tokens, feats), bf16),
                jax.ShapeDtypeStruct((feats, hidden), f32),
            ),
            in_specs=[anywhere] * 4,
            out_specs=(anywhere, anywhere),
            scratch_shapes=[
                pltpu.VMEM((tokens, feats), bf16),
                pltpu.VMEM((tokens, hidden), bf16),
                pltpu.VMEM((tokens, hidden), bf16),
                pltpu.VMEM((feats, hidden), bf16),
                pltpu.VMEM((all_tokens, hidden), bf16),
                pltpu.VMEM((feats, all_tokens), bf16),
                pltpu.VMEM((2 * NZ, tokens, feats), f32),
                pltpu.VMEM((NZ, tokens, feats), bf16),
                pltpu.VMEM((NZ, tokens, feats), bf16),
                pltpu.VMEM((2 * NZ, tokens, feats), bf16),
                pltpu.VMEM((2, 2 * NZ, tokens, feats), bf16),
                pltpu.VMEM((tokens, feats), f32),
                pltpu.VMEM((tokens, feats), bf16),
                pltpu.VMEM((3, feats, 256), f32),
                pltpu.SemaphoreType.DMA((len(NAMES),)),
                pltpu.SemaphoreType.DMA((len(NAMES),)),
                pltpu.SemaphoreType.DMA((4,)),
                pltpu.SemaphoreType.DMA((hidden // 256,)),
            ],
            compiler_params=pltpu.CompilerParams(
                collective_id=0, has_side_effects=True, vmem_limit_bytes=40 * 2**20
            ),
            cost_estimate=pl.CostEstimate(
                flops=4 * all_tokens * feats * hidden, bytes_accessed=12 * 2**20,
                transcendentals=tokens * hidden,
            ),
            name="ffn_input_backward",
        )(*(pltpu.with_memory_space_constraint(a, pltpu.HBM) for a in (inputs, pre_act, out_grad, weight)))
    )


def solution(mesh):
    in_specs = (P("mp", "dp"), P("dp", "mp"), P("dp", "mp"), P("dp", "mp"))
    out_specs = (P("mp", "dp"), P("dp", "mp"))
    return jax.shard_map(body, mesh=mesh, in_specs=in_specs, out_specs=out_specs, check_vma=False)
```

```python
import jax
import jax.numpy as jnp
from jax import lax
from jax.experimental import pallas as pl
from jax.experimental.pallas import tpu as pltpu
from jax.sharding import PartitionSpec as P

MESH = pl.DeviceIdType.MESH
gelu_scale = 0.7978845608
gelu_cubic = 0.044715

NX, NZ = 4, 8
Z_FIRST = (0, 1, 2, 3)


def gelu_slope(values):
    inner = gelu_scale * (values + gelu_cubic * values * values * values)
    tanh_part = jnp.tanh(inner)
    return 0.5 * (1.0 + tanh_part) + 0.5 * values * (1.0 - tanh_part * tanh_part) * gelu_scale * (
        1.0 + 3.0 * gelu_cubic * values * values
    )


NAMES = {}


def name_all():
    def add(*key):
        NAMES[key] = len(NAMES)

    for k in range(2):
        for kind in ("xp_own", "xm_own", "xp_yl", "xm_yl", "yl"):
            add(kind, k)
    for kind in ("xp_f", "xm_f", "xp_fy", "xm_fy"):
        add(kind)
    for q in range(8):
        add("sb", q)
    for s in range(4):
        add("al", s)
    for s in range(3):
        add("as", s)
    for i in range(8):
        add("ay", i)
    for q in range(8):
        add("ry", q)
    for q in range(64):
        add("rz", q)


name_all()


def kernel(
    inputs_hbm, pre_hbm, grad_hbm, weight_hbm, ig_hbm, wg_hbm,
    in_own, pre, grad, weight, hid, acts, kept, sent, received, z_out, z_in, own_sum, ig, wg_tile,
    send_sem, recv_sem, load_sem, store_sem,
):
    tokens = in_own.shape[0]
    feats = in_own.shape[1]
    half = tokens // 2
    pair_tokens = 2 * tokens
    col = 256
    n_cols = pre.shape[1] // col
    f_cols = feats // col

    dp, mp = lax.axis_index("dp"), lax.axis_index("mp")
    c = lax.rem(dp, 2)
    x = lax.rem(dp // 2, NX)
    yl = dp // (2 * NX)
    z = lax.rem(mp, NZ)
    yh = mp // NZ
    d = 1 - 2 * c
    other = 1 - yl
    other_row = 1 - yh

    def xat(off):
        return lax.rem(x + off + NX, NX)

    def zat(off):
        return lax.rem(z + off + NZ, NZ)

    def device(xx, lo, hi, zz, cc):
        return ((lo * NX + xx) * 2 + cc, hi * NZ + zz)

    XP = device(xat(1), yl, yh, z, c)
    XM = device(xat(-1), yl, yh, z, c)
    YL = device(x, other, yh, z, c)
    YH = device(x, yl, other_row, z, c)
    SB = device(x, yl, yh, z, 1 - c)
    ZL = device(x, yl, yh, zat(d), c)
    ZS = device(x, yl, yh, zat(-d), c)

    copies = []

    def make(key, src, dst, to, extra=0):
        i = NAMES[key] + extra
        return pltpu.make_async_remote_copy(
            src_ref=src, dst_ref=dst, send_sem=send_sem.at[i], recv_sem=recv_sem.at[i],
            device_id=to, device_id_type=MESH,
        )

    def send(key, src, to):
        copy = make(key, src, src, to)
        copy.start()
        copies.append(copy)

    def arrived(key, dst, extra=0):
        make(key, dst, dst, XP, extra).wait_recv()

    loads = [
        pltpu.make_async_copy(inputs_hbm, in_own, load_sem.at[0]),
        pltpu.make_async_copy(pre_hbm, pre, load_sem.at[1]),
        pltpu.make_async_copy(grad_hbm, grad, load_sem.at[2]),
        pltpu.make_async_copy(weight_hbm, weight, load_sem.at[3]),
    ]
    for load in loads:
        load.start()

    barrier = pltpu.get_barrier_semaphore()
    for peer in (XP, XM, YL, YH, SB, ZL, ZS):
        pl.semaphore_signal(barrier, inc=1, device_id=peer, device_id_type=MESH)

    def act(row, zz):
        at = (row * NZ + zz) * tokens
        return acts.at[:, pl.ds(pl.multiple_of(at, tokens), tokens)]

    def rows(xx, row, cc, k=None):
        at = ((row * NX + xx) * 2 + cc) * tokens
        if k is None:
            return hid.at[pl.ds(pl.multiple_of(at, tokens), tokens)]
        return hid.at[pl.ds(pl.multiple_of(at + k * half, half), half)]

    def slope_part(k):
        own = ((yl * NX + x) * 2 + c) * tokens

        @pl.loop(0, half // 16)
        def _(i):
            at = k * half + i * 16
            slope = gelu_slope(pre[pl.ds(at, 16)].astype(jnp.float32))
            value = grad[pl.ds(at, 16)].astype(jnp.float32) * slope
            hid[pl.ds(pl.multiple_of(own + at, 16), 16)] = value.astype(jnp.bfloat16)

    def send_part(k):
        mine = rows(x, yl, c, k)
        send(("yl", k), mine, YL)
        send(("xp_own", k), mine, XP)
        send(("xm_own", k), mine, XM)

    loads[1].wait()
    loads[2].wait()
    slope_part(0)
    pl.semaphore_wait(barrier, 7)
    send_part(0)
    loads[0].wait()
    act(yh, z)[...] = in_own[...].T
    send(("al", 0), act(yh, z), ZL)
    send(("as", 0), act(yh, z), ZS)
    slope_part(1)
    send_part(1)
    send(("sb", 0), rows(x, yl, c), SB)

    order = (0, 1, -1, 2)

    def sibling(q):
        send(("sb", q), rows(xat(order[q % 4]), yl if q < 4 else other, c), SB)

    def partial(q, row):
        xx = xat(order[q])
        arrived(("sb", 0), rows(xx, row, 1 - c), extra=lax.rem(row + yl, 2) * 4 + q)
        at = pl.multiple_of((row * NX + xx) * pair_tokens, pair_tokens)
        zz = 2 * xx

        @pl.loop(0, f_cols)
        def _(n):
            features = pl.ds(pl.multiple_of(n * col, col), col)
            value = lax.dot_general(
                hid[pl.ds(at, pair_tokens)], weight[features],
                (((1,), (1,)), ((), ())), preferred_element_type=jnp.float32,
            )

            def keep():
                kept[row * NZ + zz, :, features] = value[:tokens]
                kept[row * NZ + zz + 1, :, features] = value[tokens:]

            if q in Z_FIRST:
                keep()
            else:
                pl.when(row == yh)(keep)

                @pl.when(row != yh)
                def _():
                    sent[zz, :, features] = value[:tokens].astype(jnp.bfloat16)
                    sent[zz + 1, :, features] = value[tokens:].astype(jnp.bfloat16)

    def y_copy(q, b):
        at = 2 * xat(order[q]) + b
        source = z_out.at[other_row * NZ + at] if q in Z_FIRST else sent.at[at]
        return make(("ry", 2 * q + b), source, received.at[at], YH)

    def y_send(q, row):
        @pl.when(row != yh)
        def _():
            for b in range(2):
                y_copy(q, b).start()

    def act_step(s):
        block = act(yh, zat(-d * (s + 1)))
        arrived(("al", s), block)
        if s < 3:
            send(("al", s + 1), block, ZL)
            block = act(yh, zat(d * (s + 1)))
            arrived(("as", s), block)
        if s < 2:
            send(("as", s + 1), block, ZS)

    def act_partner(i, row):
        return act(row, zat(-d * i if i < 5 else d * (i - 4)))

    def act_send(i):
        send(("ay", i), act_partner(i, yh), YH)

    def acts_arrived():
        for i in range(8):
            arrived(("ay", i), act_partner(i, other_row))

    def z_place(q, b):
        at = 2 * xat(order[q]) + b
        return at, lax.rem((at - z) * d + NZ, NZ)

    def part(h):
        return pl.ds(h * half, half)

    def z_refs(q, b, h, row, short):
        at, _ = z_place(q, b)
        away = lax.rem(row + yh, 2)
        extra = 32 * away + 16 * short
        return ("rz", 4 * q + 2 * b + h), z_out.at[row * NZ + at, part(h)], z_in.at[short, row * NZ + at, part(h)], extra

    def z_copy(q, b, h, row):
        short = z_place(q, b)[1] // 5
        key, source, target, extra = z_refs(q, b, h, row, short)
        return make(key, source, target, device(x, yl, yh, zat(d * (1 - 2 * short)), c), extra)

    def z_arrived(q, b, h, row, short):
        key, _, target, extra = z_refs(q, b, h, row, short)
        arrived(key, target, extra)
        return target[...].astype(jnp.float32)

    def z_step(q, s, row):
        for b in range(2):
            at, k = z_place(q, b)
            if s < 4:
                here = (k == 5 - s) | (k == 4 + s)
            elif s == 4:
                here = k == 1
            else:
                here = k == 0

            @pl.when(here)
            def _():
                if q not in Z_FIRST:
                    arrived(("ry", 2 * q + b), received.at[at])
                for h in range(2):
                    total = kept[row * NZ + at, part(h)]
                    if q not in Z_FIRST:
                        total = total + received[at, part(h)].astype(jnp.float32)
                    if 1 < s < 5:
                        total = total + z_arrived(q, b, h, row, k // 5)
                    if s < 5:
                        z_out[row * NZ + at, part(h)] = total.astype(jnp.bfloat16)
                        z_copy(q, b, h, row).start()
                        continue
                    total = total + z_arrived(q, b, h, row, 1)
                    total = total + z_arrived(q, b, h, row, 0)
                    if q not in Z_FIRST:
                        ig[part(h)] = total.astype(jnp.bfloat16)
                        continue

                    @pl.when(row == yh)
                    def _():
                        own_sum[part(h)] = total

                    @pl.when(row != yh)
                    def _():
                        z_out[row * NZ + at, part(h)] = total.astype(jnp.bfloat16)

                if s == 5:
                    if q not in Z_FIRST:
                        pltpu.make_async_copy(ig, ig_hbm, load_sem.at[0]).start()
                    else:
                        @pl.when(row != yh)
                        def _():
                            y_copy(q, b).start()

    def finish(q):
        for b in range(2):
            at, k = z_place(q, b)

            @pl.when(k == 0)
            def _():
                arrived(("ry", 2 * q + b), received.at[at])
                ig[...] = (own_sum[...] + received[at].astype(jnp.float32)).astype(jnp.bfloat16)
                pltpu.make_async_copy(ig, ig_hbm, load_sem.at[0]).start()

    def wg_copy(n):
        columns = pl.ds(pl.multiple_of(n * col, col), col)
        return pltpu.make_async_copy(wg_tile.at[n % 3], wg_hbm.at[:, columns], store_sem.at[n])

    def tiles(first, last):
        @pl.loop(first, last)
        def _(n):
            @pl.when(n >= 3)
            def _():
                wg_copy(n - 3).wait()

            columns = pl.ds(pl.multiple_of(n * col, col), col)
            wg_tile[n % 3] = jnp.dot(acts[...], hid[:, columns], preferred_element_type=jnp.float32)
            wg_copy(n).start()

    act_step(0)
    loads[3].wait()
    partial(0, yl)
    z_step(0, 1, yl)
    act_step(1)
    for k in range(2):
        block = rows(x, other, c, k)
        arrived(("yl", k), block)
        send(("xp_yl", k), block, XP)
        send(("xm_yl", k), block, XM)
    sibling(4)
    for k in range(2):
        arrived(("xp_own", k), rows(xat(-1), yl, c, k))
        arrived(("xm_own", k), rows(xat(1), yl, c, k))
    sibling(1)
    sibling(2)
    send(("xp_f",), rows(xat(-1), yl, c, 0), XP)
    send(("xm_f",), rows(xat(1), yl, c, 1), XM)
    act_send(0)
    act_send(1)
    act_send(5)
    act_send(2)
    act_send(6)
    z_step(0, 2, yl)
    partial(1, yl)
    z_step(1, 1, yl)
    partial(2, yl)
    z_step(2, 1, yl)
    partial(0, other)
    z_step(0, 1, other)
    act_step(2)
    act_send(3)
    act_send(7)
    z_step(0, 3, yl)
    z_step(1, 2, yl)
    z_step(2, 2, yl)
    act_step(3)
    act_send(4)
    for k in range(2):
        arrived(("xp_yl", k), rows(xat(-1), other, c, k))
        arrived(("xm_yl", k), rows(xat(1), other, c, k))
        if k == 0:
            send(("xp_fy",), rows(xat(-1), other, c, 0), XP)
        else:
            send(("xm_fy",), rows(xat(1), other, c, 1), XM)
    sibling(5)
    sibling(6)
    partial(1, other)
    z_step(1, 1, other)
    partial(2, other)
    z_step(2, 1, other)
    z_step(0, 2, other)
    z_step(0, 4, yl)
    arrived(("xp_f",), rows(xat(2), yl, c, 0))
    arrived(("xm_f",), rows(xat(2), yl, c, 1))
    sibling(3)
    partial(3, yl)
    z_step(3, 1, yl)
    z_step(1, 3, yl)
    z_step(2, 3, yl)
    z_step(0, 3, other)
    z_step(0, 5, yl)
    z_step(1, 2, other)
    z_step(2, 2, other)
    arrived(("xp_fy",), rows(xat(2), other, c, 0))
    arrived(("xm_fy",), rows(xat(2), other, c, 1))
    sibling(7)
    partial(3, other)
    z_step(3, 1, other)
    z_step(3, 2, yl)
    z_step(1, 4, yl)
    z_step(2, 4, yl)
    z_step(0, 4, other)
    z_step(1, 3, other)
    z_step(2, 3, other)
    z_step(3, 3, yl)
    z_step(3, 2, other)
    acts_arrived()
    tiles(0, 1)
    z_step(1, 5, yl)
    z_step(2, 5, yl)
    z_step(0, 5, other)
    tiles(1, 2)
    z_step(1, 4, other)
    z_step(2, 4, other)
    z_step(3, 4, yl)
    z_step(3, 3, other)
    tiles(2, 4)
    z_step(1, 5, other)
    z_step(2, 5, other)
    z_step(3, 5, yl)
    tiles(4, 5)
    z_step(3, 4, other)
    tiles(5, 8)
    z_step(3, 5, other)
    tiles(8, 9)
    finish(0)
    finish(1)
    finish(2)
    finish(3)

    for copy in copies:
        copy.wait_send()
    for q in range(4):
        for b in range(2):
            _, k = z_place(q, b)
            if q not in Z_FIRST:
                y_copy(q, b).wait_send()
            else:
                @pl.when(k == 0)
                def _():
                    y_copy(q, b).wait_send()

            @pl.when(k != 0)
            def _():
                for h in range(2):
                    z_copy(q, b, h, yh).wait_send()
                    if q in Z_FIRST:
                        z_copy(q, b, h, other_row).wait_send()

    for n in range(n_cols - 3, n_cols):
        wg_copy(n).wait()
    pltpu.make_async_copy(ig, ig_hbm, load_sem.at[0]).wait()


def body(inputs, pre_act, out_grad, weight):
    tokens, feats = inputs.shape
    hidden = pre_act.shape[1]
    all_tokens = tokens * lax.axis_size("mp")
    bf16, f32 = jnp.bfloat16, jnp.float32
    anywhere = pl.BlockSpec(memory_space=pl.ANY)
    return tuple(
        pl.pallas_call(
            kernel,
            out_shape=(
                jax.ShapeDtypeStruct((tokens, feats), bf16),
                jax.ShapeDtypeStruct((feats, hidden), f32),
            ),
            in_specs=[anywhere] * 4,
            out_specs=(anywhere, anywhere),
            scratch_shapes=[
                pltpu.VMEM((tokens, feats), bf16),
                pltpu.VMEM((tokens, hidden), bf16),
                pltpu.VMEM((tokens, hidden), bf16),
                pltpu.VMEM((feats, hidden), bf16),
                pltpu.VMEM((all_tokens, hidden), bf16),
                pltpu.VMEM((feats, all_tokens), bf16),
                pltpu.VMEM((2 * NZ, tokens, feats), f32),
                pltpu.VMEM((NZ, tokens, feats), bf16),
                pltpu.VMEM((NZ, tokens, feats), bf16),
                pltpu.VMEM((2 * NZ, tokens, feats), bf16),
                pltpu.VMEM((2, 2 * NZ, tokens, feats), bf16),
                pltpu.VMEM((tokens, feats), f32),
                pltpu.VMEM((tokens, feats), bf16),
                pltpu.VMEM((3, feats, 256), f32),
                pltpu.SemaphoreType.DMA((len(NAMES),)),
                pltpu.SemaphoreType.DMA((len(NAMES),)),
                pltpu.SemaphoreType.DMA((4,)),
                pltpu.SemaphoreType.DMA((hidden // 256,)),
            ],
            compiler_params=pltpu.CompilerParams(
                collective_id=0, has_side_effects=True, vmem_limit_bytes=40 * 2**20
            ),
            cost_estimate=pl.CostEstimate(
                flops=4 * all_tokens * feats * hidden, bytes_accessed=12 * 2**20,
                transcendentals=tokens * hidden,
            ),
            name="ffn_input_backward",
        )(*(pltpu.with_memory_space_constraint(a, pltpu.HBM) for a in (inputs, pre_act, out_grad, weight)))
    )


def solution(mesh):
    in_specs = (P("mp", "dp"), P("dp", "mp"), P("dp", "mp"), P("dp", "mp"))
    out_specs = (P("mp", "dp"), P("dp", "mp"))
    return jax.shard_map(body, mesh=mesh, in_specs=in_specs, out_specs=out_specs, check_vma=False)
```
